32 devices in a mesh: node: 4 (over z), wide: 8 (over y, x, core).
Axes of the slice: x: 2, y: 2, z: 4, core: 2. Of those that a mesh axis runs over, the one named last changes fastest.
Arguments:
- tokens: bfloat16 [16384, 768], P(('node', 'wide')), may hold values from -6 to 6
- expert_index: int32 [16384, 1], P(('node', 'wide')), may hold values from 0 to 63; in each aligned block of 512 rows (0 to 511, 512 to 1023, ...) at most 16 rows name the same one
- norm_gain: float32 [768], replicated, may hold values from 0.5 to 1.5
- router_weight: float32 [768, 64], replicated, may hold values from -0.21875 to 0.21875
- expert_in: bfloat16 [64, 768, 3072], P(('node', 'wide')), may hold values from -0.21875 to 0.21875
- expert_out: bfloat16 [64, 3072, 768], P(('node', 'wide')), may hold values from -0.109375 to 0.109375
- post_gain: float32 [768], replicated, may hold values from 0.5 to 1.5
- dense_in: bfloat16 [3072, 768], P('node'), may hold values from -0.21875 to 0.21875
- scale_in: float32 [3072], P('node'), may hold values from 0.5 to 2
- dense_out: bfloat16 [3072, 768], P('node'), may hold values from -0.109375 to 0.109375
- scale_out: float32 [768], replicated, may hold values from 0.5 to 2
Outputs:
- layer_out: bfloat16 [16384, 768], P(('node', 'wide'))
The draws below stay inside these ranges and needn't reach their ends.
Inputs may be any that keep to these rules, and one draw needn't show every extreme that they name: `expert_index`: in each aligned block of 512 rows (the tokens of one device) no expert is named by more than 16 rows, a bound that some block reaches.
All inputs are finite; a program needn't handle non-finite values.
Results may differ from the reference program's by a relative error of at most 0.01.
Values may be sent and summed in bfloat16 or wider, within the bound.
A program may use at most 128 MiB of HBM per device.

```python
import math
import jax
import jax.numpy as jnp
import numpy as np
from jax import lax

D = 768
FF = 3072
TOK_DEV = 512
EXPERTS = 64
CAP = 16
TOKENS = 16384
DEVICES = 32


def shard_levels(rng, extent, cuts, low, top_value):
    def one(dim, blocks):
        heights = jax.random.uniform(jax.random.fold_in(jax.random.fold_in(rng, 6), dim), (blocks,), jnp.float32, low / len(cuts), top_value / len(cuts))
        return jnp.repeat(jnp.exp(heights), extent[dim] // blocks).reshape((-1,) + (1,) * (len(extent) - dim - 1))

    loudness = one(*cuts[0])
    for cut in cuts[1:]:
        loudness = loudness * one(*cut)
    return loudness


def shared_out(stream_key, own, number, rows, number_of, top, most, skew):
    sequence = jax.random.permutation(stream_key, number_of)
    heavy_load, usual = portions_of(number_of, rows * top, most, skew, True), portions_of(number_of, rows * top, most, skew, False)
    places = jnp.arange(number_of)

    def named(tallies, turn):
        used = int((tallies > 0).sum())
        fixed = max(1, used // 4)
        moved = fixed + (places - fixed + turn * (used - fixed)) % max(1, number_of - fixed)
        return jnp.zeros((number_of,), jnp.int32).at[sequence[jnp.where(places < fixed, places, moved)]].set(jnp.asarray(tallies, jnp.int32))

    tallies = jnp.where(number % 4 == 0, named(heavy_load, number // 4), named(usual, number - number // 4 - 1))
    mixed = jax.random.permutation(jax.random.fold_in(own, 3), number_of)
    donor, receiver = mixed[0:number_of // 2 * 2:2], mixed[1:number_of // 2 * 2:2]
    slack = jnp.minimum(tallies[donor] - 1, most - tallies[receiver]) // 2
    slack = jnp.where((donor == sequence[0]) | (receiver == sequence[0]) | (tallies[receiver] == 0), 0, jnp.maximum(slack, 0))
    moved = jax.random.randint(jax.random.fold_in(own, 4), (number_of // 2,), 0, 1 << 20) % (slack + 1)
    tallies = tallies.at[donor].add(-moved).at[receiver].add(moved)
    labels = jnp.searchsorted(jnp.cumsum(tallies), jnp.arange(rows * top), side="right").astype(jnp.int32)
    table = labels.reshape(top, rows).T
    table = table[jax.random.permutation(jax.random.fold_in(own, 1), rows)]
    turn = jax.random.randint(jax.random.fold_in(own, 2), (rows, 1), 0, top)
    return jnp.take_along_axis(table, (jnp.arange(top)[None, :] + turn) % top, axis=1)


def portions_of(number_of, total, limit, lean, full):
    loads = [(1 << 20) // math.isqrt(grade ** lean) + 1 for grade in range(1, number_of + 1)]
    largest = limit if full else min(limit, max(-(-total // number_of), total * loads[0] // sum(loads)))
    least = 1 if total - largest >= number_of - 1 else 0
    holding, spare = [largest] + [least] * (number_of - 1), total - largest - least * (number_of - 1)
    while spare > 0:
        free = [i for i in range(1, number_of) if holding[i] < largest] or [i for i in range(1, number_of) if holding[i] < limit]
        mass, budget = sum([loads[i] for i in free]), spare
        for i in free:
            more = min(limit - holding[i], max(1, budget * loads[i] // mass), spare)
            holding[i] = holding[i] + more
            spare = spare - more
    return np.array(holding)


def centred(own_key, shape, width, reach, pieces=(), kind=jnp.bfloat16):
    drawn = jax.random.normal(own_key, shape, jnp.float32) * width
    if len(pieces) > 0:
        drawn = shard_levels(own_key, shape, pieces, -0.22, 0.18) * drawn
    return jnp.clip(drawn, min=-reach, max=reach).astype(kind)


def setup_inputs(seed: int = 0) -> dict:
    arg_keys = jax.random.split(jax.random.key(seed), 12)
    tokens = centred(arg_keys[0], (TOKENS, D), 1.0, 6.0, ((0, 32),))
    expert_index_keys = jax.random.split(jax.random.fold_in(arg_keys[1], 1), TOKENS // TOK_DEV)
    expert_index_turns = jax.random.permutation(jax.random.fold_in(arg_keys[1], 3), TOKENS // TOK_DEV)
    expert_index = jax.vmap(lambda own, number: shared_out(jax.random.fold_in(arg_keys[1], 2), own, number, TOK_DEV, EXPERTS, 1, CAP, 2))(expert_index_keys, expert_index_turns).reshape((TOKENS, 1))
    norm_gain = jnp.clip(1.0 + 0.1 * jax.random.normal(arg_keys[2], (D,), jnp.float32), 0.5, 1.5)
    router_weight = centred(arg_keys[3], (D, EXPERTS), D ** -0.5, 0.21875, (), jnp.float32)
    expert_in = centred(arg_keys[4], (EXPERTS, D, FF), D ** -0.5, 0.21875, ((0, 32),))
    expert_out = centred(arg_keys[5], (EXPERTS, FF, D), FF ** -0.5, 0.109375, ((0, 32),))
    post_gain = jnp.clip(1.0 + 0.1 * jax.random.normal(arg_keys[6], (D,), jnp.float32), 0.5, 1.5)
    dense_in = centred(arg_keys[7], (FF, D), D ** -0.5, 0.21875, ((0, 4),))
    scale_in = jnp.clip(jnp.exp(math.log(2.0) - 1.3862944 * jax.random.uniform(arg_keys[8], (FF,), jnp.float32) ** shard_levels(arg_keys[8], (FF,), ((0, 4),), -0.2, 0.2)), 0.5, 2.0)
    dense_out = centred(arg_keys[9], (FF, D), FF ** -0.5, 0.109375, ((0, 4),))
    scale_out = jnp.clip(jnp.exp(jax.random.uniform(arg_keys[10], (D,), jnp.float32, math.log(0.5), math.log(2.0))), 0.5, 2.0)
    return dict(tokens=tokens, expert_index=expert_index, norm_gain=norm_gain, router_weight=router_weight, expert_in=expert_in, expert_out=expert_out, post_gain=post_gain, dense_in=dense_in, scale_in=scale_in, dense_out=dense_out, scale_out=scale_out)


def root_norm(values, gain_vector):
    floats = values.astype(jnp.float32)
    square_mean = lax.optimization_barrier(jnp.mean(floats * floats, axis=-1, keepdims=True))
    return (floats * lax.rsqrt(square_mean + 1e-06) * gain_vector).astype(jnp.bfloat16)

def reference(tokens, expert_index, norm_gain, router_weight, expert_in, expert_out, post_gain, dense_in, scale_in, dense_out, scale_out):
    normed = root_norm(tokens, norm_gain)
    chosen = expert_index[:, 0].astype(jnp.int32)
    logits = jnp.dot(normed.astype(jnp.float32), router_weight, precision=lax.Precision.HIGHEST)
    picked_logit = jnp.take_along_axis(logits, chosen[:, None], axis=1)[:, 0]
    gate_prob = 1.0 / (1.0 + jnp.exp(-picked_logit))
    expert_room = DEVICES * CAP
    counts = jnp.zeros((EXPERTS,), jnp.int32).at[chosen].add(1)
    starts = (jnp.cumsum(counts) - counts).astype(jnp.int32)
    sorted_order = jnp.argsort(chosen, stable=True).astype(jnp.int32)
    placement_index = jnp.zeros((TOKENS,), jnp.int32).at[sorted_order].set(jnp.arange(TOKENS, dtype=jnp.int32))
    expert_rank = (placement_index - starts[chosen]).astype(jnp.int32)
    ordered = jnp.concatenate([normed[sorted_order], jnp.zeros((expert_room, D), jnp.bfloat16)], axis=0)

    def one_expert(expert):
        expert_rows = lax.dynamic_slice_in_dim(ordered, starts[expert], expert_room, 0)
        hidden = jax.nn.relu(jnp.dot(expert_rows, expert_in[expert], preferred_element_type=jnp.float32)).astype(jnp.bfloat16)
        return jnp.dot(hidden, expert_out[expert], preferred_element_type=jnp.float32).astype(jnp.bfloat16)
    results = lax.map(one_expert, jnp.arange(EXPERTS, dtype=jnp.int32))
    flat_index = (chosen * expert_room + expert_rank).astype(jnp.int32)
    expert_result = results.reshape(EXPERTS * expert_room, D)[flat_index]
    residual = (tokens.astype(jnp.float32) + gate_prob[:, None] * expert_result.astype(jnp.float32)).astype(jnp.bfloat16)
    normed2 = root_norm(residual, post_gain)
    projected = lax.dot_general(normed2, dense_in, (((1,), (1,)), ((), ())), preferred_element_type=jnp.float32)
    hidden = jax.nn.relu(projected * scale_in[None, :]).astype(jnp.bfloat16)
    dense_sum = jnp.dot(hidden, dense_out, preferred_element_type=jnp.float32)
    return (residual.astype(jnp.float32) + dense_sum * scale_out[None, :]).astype(jnp.bfloat16)
```

```python
import jax
import jax.numpy as jnp
from jax import lax
from jax.sharding import PartitionSpec as P


def root_norm(values, gain_vector):
    floats = values.astype(jnp.float32)
    square_mean = jnp.mean(floats * floats, axis=-1, keepdims=True)
    return (floats * lax.rsqrt(square_mean + 1e-06) * gain_vector).astype(jnp.bfloat16)


def gather_codes(codes):
    part = codes.shape[0] // lax.axis_size("wide")
    own = lax.dynamic_slice_in_dim(codes, lax.axis_index("wide") * part, part, 0)
    return lax.all_gather(own, ("node", "wide"), axis=0, tiled=True)


def per_device(
    tokens,
    expert_index,
    norm_gain,
    router_weight,
    expert_in,
    expert_out,
    post_gain,
    dense_in,
    scale_in,
    dense_out,
    scale_out,
):
    full_in = gather_codes(dense_in)
    full_out = gather_codes(dense_out)
    full_scale = lax.all_gather(scale_in, "node", axis=0, tiled=True)
    tok_dev = tokens.shape[0]
    model_width = tokens.shape[1]
    experts = router_weight.shape[1]
    held_experts = expert_in.shape[0]
    devices = experts // held_experts
    capacity = max(2, 2 * tok_dev // experts)
    total_rows = experts * capacity
    normed = root_norm(tokens, norm_gain)
    chosen = expert_index[:, 0]
    columns = lax.broadcasted_iota(jnp.int32, (tok_dev, experts), 1)
    picked = chosen[:, None] == columns
    logits = jnp.dot(normed.astype(jnp.float32), router_weight, precision=lax.Precision.HIGHEST)
    picked_logit = jnp.sum(jnp.where(picked, logits, 0.0), axis=1)
    gate_prob = 1.0 / (1.0 + jnp.exp(-picked_logit))
    onehot = picked.astype(jnp.bfloat16)
    earlier = (
        lax.broadcasted_iota(jnp.int32, (tok_dev, tok_dev), 0)
        > lax.broadcasted_iota(jnp.int32, (tok_dev, tok_dev), 1)
    ).astype(jnp.bfloat16)
    before = jnp.dot(earlier, onehot, preferred_element_type=jnp.float32)
    slot_index = jnp.sum(jnp.where(picked, before, 0.0), axis=1).astype(jnp.int32)
    position = (
        chosen % held_experts * (devices * capacity)
        + chosen // held_experts * capacity
        + slot_index
    )
    dispatch = (
        lax.broadcasted_iota(jnp.int32, (total_rows, tok_dev), 0) == position[None, :]
    ).astype(jnp.bfloat16)
    outgoing = jnp.dot(dispatch, normed, preferred_element_type=jnp.float32).astype(jnp.bfloat16)
    packed = outgoing.reshape(held_experts, devices, capacity, model_width)
    arrived_rows = lax.all_to_all(packed, ("node", "wide"), split_axis=1, concat_axis=1, tiled=True)
    flat_rows = arrived_rows.reshape(held_experts, -1, model_width)
    hidden = jnp.einsum("jrd,jdf->jrf", flat_rows, expert_in, preferred_element_type=jnp.float32)
    hidden = jax.nn.relu(hidden).astype(jnp.bfloat16)
    produced = jnp.einsum("jrf,jfd->jrd", hidden, expert_out, preferred_element_type=jnp.float32)
    returned = lax.all_to_all(
        produced.astype(jnp.bfloat16).reshape(arrived_rows.shape),
        ("node", "wide"),
        split_axis=1,
        concat_axis=1,
        tiled=True,
    )
    expert_result = jnp.take(returned.reshape(total_rows, model_width), position, axis=0)
    residual = (
        tokens.astype(jnp.float32) + gate_prob[:, None] * expert_result.astype(jnp.float32)
    ).astype(jnp.bfloat16)
    normed2 = root_norm(residual, post_gain)
    projected = lax.dot_general(
        normed2, full_in, (((1,), (1,)), ((), ())), preferred_element_type=jnp.float32
    )
    hidden_units = jax.nn.relu(projected * full_scale[None, :]).astype(jnp.bfloat16)
    dense_sum = jnp.dot(hidden_units, full_out, preferred_element_type=jnp.float32)
    return (residual.astype(jnp.float32) + dense_sum * scale_out[None, :]).astype(jnp.bfloat16)


def solution(mesh):
    return jax.shard_map(
        per_device,
        mesh=mesh,
        in_specs=(
            P(("node", "wide"), None),
            P(("node", "wide"), None),
            P(),
            P(),
            P(("node", "wide"), None, None),
            P(("node", "wide"), None, None),
            P(),
            P("node", None),
            P("node"),
            P("node", None),
            P(),
        ),
        out_specs=P(("node", "wide"), None),
        check_vma=False,
    )
```

```python
import jax
import jax.numpy as jnp
from jax import lax
from jax.sharding import PartitionSpec as P


def root_norm(values, gain_vector):
    floats = values.astype(jnp.float32)
    square_mean = jnp.mean(floats * floats, axis=-1, keepdims=True)
    return (floats * lax.rsqrt(square_mean + 1e-06) * gain_vector).astype(jnp.bfloat16)


def gather_scale(scale):
    nodes = lax.axis_size("node")
    me = lax.axis_index("node")
    whole = jnp.zeros((nodes, scale.shape[0]), scale.dtype)
    for hop in range(nodes):
        block = scale
        if hop > 0:
            block = lax.ppermute(
                scale, "node", [(source, (source + hop) % nodes) for source in range(nodes)]
            )
        whole = lax.dynamic_update_slice_in_dim(whole, block[None], (me - hop) % nodes, 0)
    return whole


def gather_codes(codes):
    wide = lax.axis_size("wide")
    part = codes.shape[0] // wide
    own = lax.dynamic_slice_in_dim(codes, lax.axis_index("wide") * part, part, 0)
    column = lax.all_gather(own, "node", axis=0, tiled=True)
    return lax.all_gather(column, "wide", axis=0, tiled=True)


def per_device(
    tokens,
    expert_index,
    norm_gain,
    router_weight,
    expert_in,
    expert_out,
    post_gain,
    dense_in,
    scale_in,
    dense_out,
    scale_out,
):
    full_in = gather_codes(dense_in)
    full_out = gather_codes(dense_out)
    wide = lax.axis_size("wide")
    scale_parts = gather_scale(scale_in).reshape(lax.axis_size("node"), wide, -1)
    full_scale = scale_parts.transpose(1, 0, 2).reshape(-1)
    tok_dev = tokens.shape[0]
    model_width = tokens.shape[1]
    experts = router_weight.shape[1]
    held_experts = expert_in.shape[0]
    devices = experts // held_experts
    capacity = max(2, 2 * tok_dev // experts)
    total_rows = experts * capacity
    normed = root_norm(tokens, norm_gain)
    chosen = expert_index[:, 0]
    columns = lax.broadcasted_iota(jnp.int32, (tok_dev, experts), 1)
    picked = chosen[:, None] == columns
    logits = jnp.dot(normed.astype(jnp.float32), router_weight, precision=lax.Precision.HIGHEST)
    picked_logit = jnp.sum(jnp.where(picked, logits, 0.0), axis=1)
    gate_prob = 1.0 / (1.0 + jnp.exp(-picked_logit))
    onehot = picked.astype(jnp.bfloat16)
    earlier = (
        lax.broadcasted_iota(jnp.int32, (tok_dev, tok_dev), 0)
        > lax.broadcasted_iota(jnp.int32, (tok_dev, tok_dev), 1)
    ).astype(jnp.bfloat16)
    before = jnp.dot(earlier, onehot, preferred_element_type=jnp.float32)
    slot_index = jnp.sum(jnp.where(picked, before, 0.0), axis=1).astype(jnp.int32)
    position = (
        chosen % held_experts * (devices * capacity)
        + chosen // held_experts * capacity
        + slot_index
    )
    dispatch = (
        lax.broadcasted_iota(jnp.int32, (total_rows, tok_dev), 0) == position[None, :]
    ).astype(jnp.bfloat16)
    outgoing = jnp.dot(dispatch, normed, preferred_element_type=jnp.float32).astype(jnp.bfloat16)
    packed = outgoing.reshape(held_experts, devices, capacity, model_width)
    arrived_rows = lax.all_to_all(packed, ("node", "wide"), split_axis=1, concat_axis=1, tiled=True)
    flat_rows = arrived_rows.reshape(held_experts, -1, model_width)
    hidden = jnp.einsum("jrd,jdf->jrf", flat_rows, expert_in, preferred_element_type=jnp.float32)
    hidden = jax.nn.relu(hidden).astype(jnp.bfloat16)
    produced = jnp.einsum("jrf,jfd->jrd", hidden, expert_out, preferred_element_type=jnp.float32)
    returned = lax.all_to_all(
        produced.astype(jnp.bfloat16).reshape(arrived_rows.shape),
        ("node", "wide"),
        split_axis=1,
        concat_axis=1,
        tiled=True,
    )
    expert_result = jnp.take(returned.reshape(total_rows, model_width), position, axis=0)
    residual = (
        tokens.astype(jnp.float32) + gate_prob[:, None] * expert_result.astype(jnp.float32)
    ).astype(jnp.bfloat16)
    normed2 = root_norm(residual, post_gain)
    projected = lax.dot_general(
        normed2, full_in, (((1,), (1,)), ((), ())), preferred_element_type=jnp.float32
    )
    hidden_units = jax.nn.relu(projected * full_scale[None, :]).astype(jnp.bfloat16)
    dense_sum = jnp.dot(hidden_units, full_out, preferred_element_type=jnp.float32)
    return (residual.astype(jnp.float32) + dense_sum * scale_out[None, :]).astype(jnp.bfloat16)


def solution(mesh):
    return jax.shard_map(
        per_device,
        mesh=mesh,
        in_specs=(
            P(("node", "wide"), None),
            P(("node", "wide"), None),
            P(),
            P(),
            P(("node", "wide"), None, None),
            P(("node", "wide"), None, None),
            P(),
            P("node", None),
            P("node"),
            P("node", None),
            P(),
        ),
        out_specs=P(("node", "wide"), None),
        check_vma=False,
    )
```

```python
import jax
import jax.numpy as jnp
from jax import lax
from jax.sharding import PartitionSpec as P


def root_norm(values, gain_vector):
    floats = values.astype(jnp.float32)
    square_mean = jnp.mean(floats * floats, axis=-1, keepdims=True)
    return (floats * lax.rsqrt(square_mean + 1e-06) * gain_vector).astype(jnp.bfloat16)


def gather_scale(scale):
    nodes = lax.axis_size("node")
    me = lax.axis_index("node")
    whole = jnp.zeros((nodes, scale.shape[0]), scale.dtype)
    for hop in range(nodes):
        block = scale
        if hop > 0:
            block = lax.ppermute(
                scale, "node", [(source, (source + hop) % nodes) for source in range(nodes)]
            )
        whole = lax.dynamic_update_slice_in_dim(whole, block[None], (me - hop) % nodes, 0)
    return whole


def gather_codes(codes):
    wide = lax.axis_size("wide")
    part = codes.shape[0] // wide
    own = lax.dynamic_slice_in_dim(codes, lax.axis_index("wide") * part, part, 0)
    column = lax.all_gather(own, "node", axis=0, tiled=True)
    return lax.all_gather(column, "wide", axis=0, tiled=True)


def per_device(
    tokens,
    expert_index,
    norm_gain,
    router_weight,
    expert_in,
    expert_out,
    post_gain,
    dense_in,
    scale_in,
    dense_out,
    scale_out,
):
    codes = gather_codes(jnp.concatenate([dense_in, dense_out], axis=1))
    full_in, full_out = codes[:, : dense_in.shape[1]], codes[:, dense_in.shape[1] :]
    wide = lax.axis_size("wide")
    scale_parts = gather_scale(scale_in).reshape(lax.axis_size("node"), wide, -1)
    full_scale = scale_parts.transpose(1, 0, 2).reshape(-1)
    tok_dev = tokens.shape[0]
    model_width = tokens.shape[1]
    experts = router_weight.shape[1]
    held_experts = expert_in.shape[0]
    devices = experts // held_experts
    capacity = max(2, 2 * tok_dev // experts)
    total_rows = experts * capacity
    normed = root_norm(tokens, norm_gain)
    chosen = expert_index[:, 0]
    columns = lax.broadcasted_iota(jnp.int32, (tok_dev, experts), 1)
    picked = chosen[:, None] == columns
    logits = jnp.dot(normed.astype(jnp.float32), router_weight, precision=lax.Precision.HIGHEST)
    picked_logit = jnp.sum(jnp.where(picked, logits, 0.0), axis=1)
    gate_prob = 1.0 / (1.0 + jnp.exp(-picked_logit))
    onehot = picked.astype(jnp.bfloat16)
    earlier = (
        lax.broadcasted_iota(jnp.int32, (tok_dev, tok_dev), 0)
        > lax.broadcasted_iota(jnp.int32, (tok_dev, tok_dev), 1)
    ).astype(jnp.bfloat16)
    before = jnp.dot(earlier, onehot, preferred_element_type=jnp.float32)
    slot_index = jnp.sum(jnp.where(picked, before, 0.0), axis=1).astype(jnp.int32)
    position = (
        chosen % held_experts * (devices * capacity)
        + chosen // held_experts * capacity
        + slot_index
    )
    dispatch = (
        lax.broadcasted_iota(jnp.int32, (total_rows, tok_dev), 0) == position[None, :]
    ).astype(jnp.bfloat16)
    outgoing = jnp.dot(dispatch, normed, preferred_element_type=jnp.float32).astype(jnp.bfloat16)
    packed = outgoing.reshape(held_experts, devices, capacity, model_width)
    arrived_rows = lax.all_to_all(packed, ("node", "wide"), split_axis=1, concat_axis=1, tiled=True)
    flat_rows = arrived_rows.reshape(held_experts, -1, model_width)
    hidden = jnp.einsum("jrd,jdf->jrf", flat_rows, expert_in, preferred_element_type=jnp.float32)
    hidden = jax.nn.relu(hidden).astype(jnp.bfloat16)
    produced = jnp.einsum("jrf,jfd->jrd", hidden, expert_out, preferred_element_type=jnp.float32)
    returned = lax.all_to_all(
        produced.astype(jnp.bfloat16).reshape(arrived_rows.shape),
        ("node", "wide"),
        split_axis=1,
        concat_axis=1,
        tiled=True,
    )
    expert_result = jnp.take(returned.reshape(total_rows, model_width), position, axis=0)
    residual = (
        tokens.astype(jnp.float32) + gate_prob[:, None] * expert_result.astype(jnp.float32)
    ).astype(jnp.bfloat16)
    normed2 = root_norm(residual, post_gain)
    projected = lax.dot_general(
        normed2, full_in, (((1,), (1,)), ((), ())), preferred_element_type=jnp.float32
    )
    hidden_units = jax.nn.relu(projected * full_scale[None, :]).astype(jnp.bfloat16)
    dense_sum = jnp.dot(hidden_units, full_out, preferred_element_type=jnp.float32)
    return (residual.astype(jnp.float32) + dense_sum * scale_out[None, :]).astype(jnp.bfloat16)


def solution(mesh):
    return jax.shard_map(
        per_device,
        mesh=mesh,
        in_specs=(
            P(("node", "wide"), None),
            P(("node", "wide"), None),
            P(),
            P(),
            P(("node", "wide"), None, None),
            P(("node", "wide"), None, None),
            P(),
            P("node", None),
            P("node"),
            P("node", None),
            P(),
        ),
        out_specs=P(("node", "wide"), None),
        check_vma=False,
    )
```
